768 devices in a mesh: dp: 64 (over y, z_hi, core), blk: 12 (over z_lo, x).
Axes of the slice: x: 4, y: 8, z: 12 (z_hi: 4, z_lo: 3; z = z_hi * 3 + z_lo), core: 2. Of those that a mesh axis runs over, the one named last changes fastest.
Arguments:
- tokens: bfloat16 [98304, 6144], P('dp', 'blk'), may hold values from -6 to 6
- key_grad: bfloat16 [98304, 512], P(('dp', 'blk')), may hold values from -6 to 6
- weight: float32 [6144, 512], P('blk'), may hold values from -6 to 6
- moment: float32 [6144, 512], P('blk'), may hold values from -6 to 6
- second: float32 [6144, 512], P('blk'), may hold values from 0.5 to 20
Outputs:
- keys: bfloat16 [98304, 512], P(('dp', 'blk'))
- token_grad: bfloat16 [98304, 6144], P('dp', 'blk')
- weight_grad: float32 [6144, 512], P('blk')
- weight_new: float32 [6144, 512], P('blk')
- moment_new: float32 [6144, 512], P('blk')
- second_new: float32 [6144, 512], P('blk')
The draws below stay inside these ranges and needn't reach their ends.
All inputs are finite; a program needn't handle non-finite values.
Results may differ from the reference program's by a relative error of at most 0.0049.
Values may be sent and summed in bfloat16 or wider, within the bound.
No kernel may reach another device: no remote copies, remote signals or barrier semaphores. Data moves between devices by JAX's collectives and lax.ppermute only.
A program may use at most 64 MiB of HBM per device.

```python
import math
import jax
import jax.numpy as jnp

D = 6144
STEP = 100
WIDTH = 512
TOKENS = 98304


def block_scale(key, dims, pieces, least, top_value):
    loudness, own = 1.0, jax.random.fold_in(key, 6)
    for axis_at, blocks in pieces:
        heights = jnp.exp(jax.random.uniform(jax.random.fold_in(own, axis_at), (blocks,), jnp.float32, least / len(pieces), top_value / len(pieces)))
        loudness = loudness * jnp.repeat(heights, dims[axis_at] // blocks).reshape([-1 if axis == axis_at else 1 for axis in range(len(dims))])
    return loudness


def noise(stream_key, dims, deviation, limit, shards=(), held_as=jnp.bfloat16):
    result = jax.random.normal(stream_key, dims, jnp.float32) * deviation
    if len(shards) > 0:
        result = block_scale(stream_key, dims, shards, -0.22, 0.18) * result
    return jnp.clip(result, min=-limit, max=limit).astype(held_as)


def setup_inputs(seed: int = 0) -> dict:
    seeds = jax.random.split(jax.random.key(seed), 6)
    tokens = noise(seeds[0], (TOKENS, D), 1.0, 6.0, ((0, 64), (1, 12)))
    key_grad = noise(seeds[1], (TOKENS, WIDTH), 1.0, 6.0, ((0, 768),))
    weight = noise(seeds[2], (D, WIDTH), 1.0, 6.0, ((0, 12),), jnp.float32)
    moment = noise(seeds[3], (D, WIDTH), 0.5, 6.0, ((0, 12),), jnp.float32)
    second = jnp.clip(jnp.exp(math.log(20.0) - 3.6888795 * jax.random.uniform(seeds[4], (D, WIDTH), jnp.float32) ** block_scale(seeds[4], (D, WIDTH), ((0, 12),), -0.2, 0.2)), 0.5, 20.0)
    return {"tokens": tokens, "key_grad": key_grad, "weight": weight, "moment": moment, "second": second}


def reference(tokens, key_grad, weight, moment, second):
    factor = D ** (-0.5)
    scaled = (weight * factor).astype(jnp.bfloat16)
    keys = jnp.dot(tokens, scaled, preferred_element_type=jnp.float32).astype(jnp.bfloat16)
    token_grad = jnp.dot(key_grad, scaled.T, preferred_element_type=jnp.float32).astype(jnp.bfloat16)
    weight_grad = jnp.dot(tokens.T, key_grad, preferred_element_type=jnp.float32) * factor
    moment_new = 0.9 * moment + 0.1 * weight_grad
    second_new = 0.999 * second + 0.001 * weight_grad * weight_grad
    first_fix = 1.0 - 0.9 ** STEP
    second_fix = 1.0 - 0.999 ** STEP
    step_dir = moment_new / first_fix / (jnp.sqrt(second_new / second_fix) + 1e-08)
    weight_new = weight - 0.05 * (step_dir + 0.1 * weight)
    return (keys, token_grad, weight_grad, weight_new, moment_new, second_new)
```

```python
import jax
import jax.numpy as jnp
from jax import lax
from jax.experimental import pallas as pl
from jax.experimental.pallas import tpu as pltpu
from jax.sharding import Mesh, PartitionSpec as P

D = 6144
STEP = 100
FACTOR = D ** (-0.5)
AXES = ("y", "zh", "c", "zl", "x")
DP = ("y", "zh", "c")
BLK = ("zl", "x")
PAIR = ("c", "y")
BF16, F32 = jnp.bfloat16, jnp.float32
VMEM = pl.BlockSpec(memory_space=pltpu.VMEM)
SMEM = pl.BlockSpec(memory_space=pltpu.SMEM)
ANY = pl.BlockSpec(memory_space=pl.ANY)


def optimize(weight, moment, second, weight_grad):
    moment_new = 0.9 * moment + 0.1 * weight_grad
    second_new = 0.999 * second + 0.001 * weight_grad * weight_grad
    first_fix = 1.0 - 0.9**STEP
    second_fix = 1.0 - 0.999**STEP
    step_dir = moment_new / first_fix / (jnp.sqrt(second_new / second_fix) + 1e-08)
    weight_new = weight - 0.05 * (step_dir + 0.1 * weight)
    return (weight_new, moment_new, second_new)


def params(mib):
    return pltpu.CompilerParams(vmem_limit_bytes=mib << 20)


def cost(flops, nbytes):
    return pl.CostEstimate(flops=flops, bytes_accessed=nbytes, transcendentals=0)


def like(shape, dtype=BF16):
    return jax.ShapeDtypeStruct(shape, dtype)


def swap_parts(x, axes):
    return lax.all_to_all(x, axes, 0, 0, tiled=True)


def copies_kernel(x_ref, o_ref, sem):
    count = o_ref.shape[0]
    copies = [pltpu.make_async_copy(x_ref, o_ref.at[i], sem.at[i]) for i in range(count)]
    for copy in copies:
        copy.start()
    for copy in copies:
        copy.wait()


def copies_of(x, count):
    return pl.pallas_call(
        copies_kernel,
        out_shape=like((count,) + x.shape, x.dtype),
        in_specs=[VMEM],
        out_specs=ANY,
        scratch_shapes=[pltpu.SemaphoreType.DMA((count,))],
        compiler_params=params(4),
        cost_estimate=cost(0, x.size * 2 * (count + 1)),
    )(x)


def sum_copies_kernel(x_ref, o_ref):
    total = x_ref[0].astype(F32)
    for i in range(1, x_ref.shape[0]):
        total = total + x_ref[i].astype(F32)
    total = total.astype(o_ref.dtype)
    for i in range(o_ref.shape[0]):
        o_ref[i] = total


def sum_copies(x, count):
    return pl.pallas_call(
        sum_copies_kernel,
        out_shape=like((count,) + x.shape[1:]),
        in_specs=[VMEM],
        out_specs=VMEM,
        compiler_params=params(4),
        cost_estimate=cost(x.size, x.size * 2),
    )(x)


def partial_kernel(me_ref, tokens_ref, weight_ref, *outs):
    count = len(outs)
    groups = 3
    rows = tokens_ref.shape[0] // (count * groups)
    scaled = (weight_ref[...] * FACTOR).astype(BF16)
    for shift, out in enumerate(outs):
        at = lax.rem(me_ref[0] + shift, count)
        block = jnp.concatenate(
            [tokens_ref[pl.ds(pl.multiple_of((g * count + at) * rows, rows), rows), :] for g in range(groups)], 0
        )
        out[...] = jnp.dot(block, scaled, preferred_element_type=F32).astype(out.dtype)


def partial_keys(tokens, weight, count):
    rows, width = tokens.shape[0] // count, weight.shape[1]
    return pl.pallas_call(
        partial_kernel,
        out_shape=[like((rows, width))] * count,
        in_specs=[SMEM, VMEM, VMEM],
        out_specs=[VMEM] * count,
        compiler_params=params(16),
        cost_estimate=cost(2 * tokens.size * width, 4 << 20),
    )(lax.axis_index("x").reshape(1), tokens, weight)


def hold_kernel(*refs):
    pass


def hold_until(xs, dep):
    count = len(xs)
    return pl.pallas_call(
        hold_kernel,
        out_shape=[like(x.shape, x.dtype) for x in xs],
        in_specs=[ANY] * (count + 1),
        out_specs=[ANY] * count,
        input_output_aliases={i: i for i in range(count)},
        cost_estimate=cost(0, 0),
        compiler_params=params(1),
    )(*xs, dep)


def ring_sum_kernel(me_ref, *refs):
    parts, outs = refs[:-3], refs[-3:]
    count = len(outs)
    rows = outs[0].shape[0]
    for shift, out in enumerate(outs):
        at = pl.ds(pl.multiple_of(lax.rem(me_ref[0] + shift, count) * rows, rows), rows)
        total = parts[0][at, :].astype(F32)
        for part in parts[1:]:
            total = total + part[at, :].astype(F32)
        out[...] = total.astype(out.dtype)


def ring_sum(parts):
    rows, width = parts[0].shape
    return pl.pallas_call(
        ring_sum_kernel,
        out_shape=[like((rows // 3, width), F32)] + [like((rows // 3, width))] * 2,
        in_specs=[SMEM] + [VMEM] * len(parts),
        out_specs=[VMEM] * 3,
        compiler_params=params(8),
        cost_estimate=cost(4 * rows * width, 4 << 20),
    )(lax.axis_index("zl").reshape(1), *parts)


def send(x, axis, shift):
    count = lax.axis_size(axis)
    return lax.ppermute(x, axis, [(i, (i + shift) % count) for i in range(count)])


def back_kernel(piece_ref, weight_ref, o_ref, scaled_ref):
    @pl.when(pl.program_id(0) == 0)
    def _():
        scaled_ref[...] = (weight_ref[...] * FACTOR).astype(BF16)

    o_ref[...] = lax.dot_general(
        piece_ref[...], scaled_ref[...], (((1,), (1,)), ((), ())), preferred_element_type=F32
    ).astype(o_ref.dtype)


def token_gradient(piece, weight):
    rows, width = piece.shape
    feats = weight.shape[0]
    tile = 256
    return pl.pallas_call(
        back_kernel,
        out_shape=like((rows, feats)),
        grid=(rows // tile,),
        in_specs=[pl.BlockSpec((tile, width), lambda i: (i, 0)), pl.BlockSpec((feats, width), lambda i: (0, 0))],
        out_specs=pl.BlockSpec((tile, feats), lambda i: (i, 0)),
        scratch_shapes=[pltpu.VMEM((feats, width), BF16)],
        compiler_params=params(16),
        cost_estimate=cost(2 * rows * width * feats, 4 << 20),
    )(piece, weight)


def local(tokens, key_grad, weight, moment, second):
    rows, width, feats = tokens.shape[0], key_grad.shape[1], tokens.shape[1]
    size = lax.axis_size
    piece = swap_parts(copies_of(key_grad, size("zl") * size("x")), BLK).reshape(rows, width)
    own, *out = partial_keys(tokens, weight, size("x"))

    grad = lax.dot_general(tokens, piece, (((0,), (0,)), ((), ())), preferred_element_type=F32) * FACTOR
    grad = grad.astype(BF16)
    pair = size("y") * size("c")
    shares = swap_parts(grad.reshape(pair, feats // pair, width), PAIR)
    shares = swap_parts(sum_copies(shares, size("zh")), "zh")
    half = swap_parts(sum_copies(shares, size("y")), "y").reshape(feats // size("c"), width)
    weight_grad = lax.all_gather(half, "c", axis=0, tiled=True).astype(F32)

    out = hold_until(out, grad)
    got = [send(x, "x", 1 + i) for i, x in enumerate(out)]
    mine, *out = ring_sum([own] + got)
    got = [send(x, "zl", 1 + i) for i, x in enumerate(out)]
    keys = (mine + got[0].astype(F32) + got[1].astype(F32)).astype(BF16)

    back = token_gradient(piece, weight)
    weight_new, moment_new, second_new = optimize(weight, moment, second, weight_grad)
    return (keys, back, weight_grad, weight_new, moment_new, second_new)


def solution(mesh):
    fine = Mesh(mesh.devices.reshape(8, 4, 2, 3, 4), AXES)
    in_specs = (P(DP, BLK), P(DP + BLK, None), P(BLK, None), P(BLK, None), P(BLK, None))
    out_specs = (P(DP + BLK, None), P(DP, BLK), P(BLK, None), P(BLK, None), P(BLK, None), P(BLK, None))
    return jax.shard_map(local, mesh=fine, in_specs=in_specs, out_specs=out_specs, check_vma=False)
```

```python
import jax
import jax.numpy as jnp
from jax import lax
from jax.experimental import pallas as pl
from jax.experimental.pallas import tpu as pltpu
from jax.sharding import Mesh, PartitionSpec as P

D = 6144
STEP = 100
FACTOR = D ** (-0.5)
AXES = ("y", "zh", "c", "zl", "x")
DP = ("y", "zh", "c")
BLK = ("zl", "x")
PAIR = ("c", "y")
BRIEF = pl.CostEstimate(flops=1, bytes_accessed=1, transcendentals=0)
BF16, F32 = jnp.bfloat16, jnp.float32
VMEM = pl.BlockSpec(memory_space=pltpu.VMEM)
SMEM = pl.BlockSpec(memory_space=pltpu.SMEM)
ANY = pl.BlockSpec(memory_space=pl.ANY)


def optimize(weight, moment, second, weight_grad):
    moment_new = 0.9 * moment + 0.1 * weight_grad
    second_new = 0.999 * second + 0.001 * weight_grad * weight_grad
    first_fix = 1.0 / (1.0 - 0.9**STEP)
    second_fix = 1.0 / (1.0 - 0.999**STEP)
    step_dir = moment_new * first_fix / (jnp.sqrt(second_new * second_fix) + 1e-08)
    weight_new = weight - 0.05 * (step_dir + 0.1 * weight)
    return (weight_new, moment_new, second_new)


def params(mib):
    return pltpu.CompilerParams(vmem_limit_bytes=mib << 20)


def like(shape, dtype=BF16):
    return jax.ShapeDtypeStruct(shape, dtype)


TOKEN = like((8, 128), F32)


def swap_parts(x, axes):
    return lax.all_to_all(x, axes, 0, 0, tiled=True)


def copies_kernel(x_ref, o_ref):
    for i in range(o_ref.shape[0]):
        o_ref[i] = x_ref[...]


def copies_of(x, count):
    return pl.pallas_call(
        copies_kernel,
        out_shape=like((count,) + x.shape, x.dtype),
        in_specs=[VMEM],
        out_specs=VMEM,
        compiler_params=params(4),
        cost_estimate=BRIEF,
    )(x)


def sum_copies_kernel(x_ref, *refs):
    o_ref, token_ref = refs[-2:]
    total = x_ref[0].astype(F32)
    for i in range(1, x_ref.shape[0]):
        total = total + x_ref[i].astype(F32)
    total = total.astype(o_ref.dtype)
    for i in range(o_ref.shape[0]):
        o_ref[i] = total
    token_ref[...] = jnp.zeros(token_ref.shape, F32)


def sum_copies(x, count, *tokens):
    return pl.pallas_call(
        sum_copies_kernel,
        out_shape=[like((count,) + x.shape[1:]), TOKEN],
        in_specs=[VMEM] + [ANY] * len(tokens),
        out_specs=[VMEM] * 2,
        compiler_params=params(4),
        cost_estimate=BRIEF,
    )(x, *tokens)


def partial_kernel(me_ref, tokens_ref, weight_ref, dep_ref, *outs):
    count = len(outs)
    groups = 3
    rows = tokens_ref.shape[0] // (count * groups)
    scaled = (weight_ref[...] * FACTOR).astype(BF16)
    for shift, out in enumerate(outs):
        at = lax.rem(me_ref[0] + shift, count)
        block = jnp.concatenate(
            [tokens_ref[pl.ds(pl.multiple_of((g * count + at) * rows, rows), rows), :] for g in range(groups)], 0
        )
        out[...] = jnp.dot(block, scaled, preferred_element_type=F32).astype(out.dtype)


def partial_keys(tokens, weight, count, dep):
    rows, width = tokens.shape[0] // count, weight.shape[1]
    return pl.pallas_call(
        partial_kernel,
        out_shape=[like((rows, width))] * count,
        in_specs=[SMEM, VMEM, VMEM, ANY],
        out_specs=[VMEM] * count,
        compiler_params=params(16),
        cost_estimate=BRIEF,
    )(lax.axis_index("x").reshape(1), tokens, weight, dep)


def ring_sum_kernel(me_ref, after_ref, *refs):
    parts, outs, token_ref = refs[:-4], refs[-4:-1], refs[-1]
    token_ref[...] = jnp.zeros(token_ref.shape, F32)
    count = len(outs)
    rows = outs[0].shape[0]
    for shift, out in enumerate(outs):
        at = pl.ds(pl.multiple_of(lax.rem(me_ref[0] + shift, count) * rows, rows), rows)
        total = parts[0][at, :].astype(F32)
        for part in parts[1:]:
            total = total + part[at, :].astype(F32)
        out[...] = total.astype(out.dtype)


def ring_sum(parts, token):
    rows, width = parts[0].shape
    return pl.pallas_call(
        ring_sum_kernel,
        out_shape=[like((rows // 3, width), F32)] + [like((rows // 3, width))] * 2 + [TOKEN],
        in_specs=[SMEM, ANY] + [VMEM] * len(parts),
        out_specs=[VMEM] * 4,
        compiler_params=params(8),
        cost_estimate=BRIEF,
    )(lax.axis_index("zl").reshape(1), token, *parts)


def finish_kernel(g_ref, weight_ref, moment_ref, second_ref, a_ref, b_ref, c_ref, *outs):
    grad = g_ref[...].astype(F32)
    new = optimize(weight_ref[...], moment_ref[...], second_ref[...], grad)
    keys = (a_ref[...] + b_ref[...].astype(F32) + c_ref[...].astype(F32)).astype(BF16)
    for out, value in zip(outs, (keys, grad) + new, strict=True):
        out[...] = value


def finish(grad, weight, moment, second, parts):
    (rows, width), (few, _) = grad.shape, parts[0].shape
    steps = 4
    big = pl.BlockSpec((rows // steps, width), lambda i: (i, 0))
    small = pl.BlockSpec((few // steps, width), lambda i: (i, 0))
    return pl.pallas_call(
        finish_kernel,
        out_shape=[like((few, width))] + [like((rows, width), F32)] * 4,
        grid=(steps,),
        in_specs=[big] * 4 + [small] * 3,
        out_specs=[small] + [big] * 4,
        compiler_params=params(16),
        cost_estimate=BRIEF,
    )(grad, weight, moment, second, *parts)


def send(x, axis, shift):
    count = lax.axis_size(axis)
    return lax.ppermute(x, axis, [(i, (i + shift) % count) for i in range(count)])


def back_kernel(after_ref, piece_ref, weight_ref, o_ref, token_ref, scaled_ref):
    @pl.when(pl.program_id(0) == 0)
    def _():
        scaled_ref[...] = (weight_ref[...] * FACTOR).astype(BF16)
        token_ref[...] = jnp.zeros(token_ref.shape, F32)

    o_ref[...] = lax.dot_general(
        piece_ref[...], scaled_ref[...], (((1,), (1,)), ((), ())), preferred_element_type=F32
    ).astype(o_ref.dtype)


def token_gradient(piece, weight, token):
    rows, width = piece.shape
    feats = weight.shape[0]
    tile = 512
    return pl.pallas_call(
        back_kernel,
        out_shape=[like((rows, feats)), TOKEN],
        grid=(rows // tile,),
        in_specs=[
            ANY,
            pl.BlockSpec((tile, width), lambda i: (i, 0)),
            pl.BlockSpec((feats, width), lambda i: (0, 0)),
        ],
        out_specs=[pl.BlockSpec((tile, feats), lambda i: (i, 0)), pl.BlockSpec((8, 128), lambda i: (0, 0))],
        scratch_shapes=[pltpu.VMEM((feats, width), BF16)],
        compiler_params=params(16),
        cost_estimate=BRIEF,
    )(token, piece, weight)


def local(tokens, key_grad, weight, moment, second):
    rows, width, feats = tokens.shape[0], key_grad.shape[1], tokens.shape[1]
    size = lax.axis_size
    piece = swap_parts(copies_of(key_grad, size("zl") * size("x")), BLK).reshape(rows, width)

    grad = lax.dot_general(tokens, piece, (((0,), (0,)), ((), ())), preferred_element_type=F32) * FACTOR
    grad = grad.astype(BF16)
    own, *out = partial_keys(tokens, weight, size("x"), grad)
    got = [send(x, "x", 1 + i) for i, x in enumerate(out)]
    pair = size("y") * size("c")
    shares, first = sum_copies(swap_parts(grad.reshape(pair, feats // pair, width), PAIR), size("zh"))
    back, after_back = token_gradient(piece, weight, first)
    mine, *out, after_keys = ring_sum([own] + got, first)
    got = [send(x, "zl", 1 + i) for i, x in enumerate(out)]
    shares, _ = sum_copies(swap_parts(shares, "zh"), size("y"), after_back, after_keys)
    half = swap_parts(shares, "y").reshape(feats // size("c"), width)
    full = lax.all_gather(half, "c", axis=0, tiled=True)
    keys, weight_grad, *new = finish(full, weight, moment, second, [mine] + got)
    return (keys, back, weight_grad, *new)


def solution(mesh):
    fine = Mesh(mesh.devices.reshape(8, 4, 2, 3, 4), AXES)
    in_specs = (P(DP, BLK), P(DP + BLK, None), P(BLK, None), P(BLK, None), P(BLK, None))
    out_specs = (P(DP + BLK, None), P(DP, BLK), P(BLK, None), P(BLK, None), P(BLK, None), P(BLK, None))
    return jax.shard_map(local, mesh=fine, in_specs=in_specs, out_specs=out_specs, check_vma=False)
```

```python
import jax
import jax.numpy as jnp
from jax import lax
from jax.experimental import pallas as pl
from jax.experimental.pallas import tpu as pltpu
from jax.sharding import Mesh, PartitionSpec as P

D = 6144
STEP = 100
FACTOR = D ** (-0.5)
AXES = ("y", "zh", "c", "zl", "x")
DP = ("y", "zh", "c")
BLK = ("zl", "x")
BRIEF = pl.CostEstimate(flops=1, bytes_accessed=1, transcendentals=0)
BF16, F32 = jnp.bfloat16, jnp.float32
VMEM = pl.BlockSpec(memory_space=pltpu.VMEM)
SMEM = pl.BlockSpec(memory_space=pltpu.SMEM)
ANY = pl.BlockSpec(memory_space=pl.ANY)


def optimize(weight, moment, second, weight_grad):
    moment_new = 0.9 * moment + 0.1 * weight_grad
    second_new = 0.999 * second + 0.001 * weight_grad * weight_grad
    first_fix = 1.0 / (1.0 - 0.9**STEP)
    second_fix = 1.0 / (1.0 - 0.999**STEP)
    step_dir = moment_new * first_fix / (jnp.sqrt(second_new * second_fix) + 1e-08)
    weight_new = weight - 0.05 * (step_dir + 0.1 * weight)
    return (weight_new, moment_new, second_new)


def params(mib):
    return pltpu.CompilerParams(vmem_limit_bytes=mib << 20)


def like(shape, dtype=BF16):
    return jax.ShapeDtypeStruct(shape, dtype)


TOKEN = like((8, 128), F32)


def swap_parts(x, axes):
    return lax.all_to_all(x, axes, 0, 0, tiled=True)


def copies_kernel(x_ref, o_ref):
    for i in range(o_ref.shape[0]):
        o_ref[i] = x_ref[...]


def copies_of(x, count):
    return pl.pallas_call(
        copies_kernel,
        out_shape=like((count,) + x.shape, x.dtype),
        in_specs=[VMEM],
        out_specs=VMEM,
        compiler_params=params(4),
        cost_estimate=BRIEF,
    )(x)


def sum_copies_kernel(x_ref, *refs):
    o_ref, token_ref = refs[-2:]
    total = x_ref[0].astype(F32)
    for i in range(1, x_ref.shape[0]):
        total = total + x_ref[i].astype(F32)
    total = total.astype(o_ref.dtype)
    for i in range(o_ref.shape[0]):
        o_ref[i] = total
    token_ref[...] = jnp.zeros(token_ref.shape, F32)


def sum_copies(x, count, *tokens):
    return pl.pallas_call(
        sum_copies_kernel,
        out_shape=[like((count,) + x.shape[1:]), TOKEN],
        in_specs=[VMEM] + [ANY] * len(tokens),
        out_specs=[VMEM] * 2,
        compiler_params=params(4),
        cost_estimate=BRIEF,
    )(x, *tokens)


def partial_kernel(me_ref, tokens_ref, weight_ref, *outs):
    count = len(outs)
    groups = 3
    rows = tokens_ref.shape[0] // (count * groups)
    scaled = (weight_ref[...] * FACTOR).astype(BF16)
    for shift, out in enumerate(outs):
        at = lax.rem(me_ref[0] + shift, count)
        block = jnp.concatenate(
            [tokens_ref[pl.ds(pl.multiple_of((g * count + at) * rows, rows), rows), :] for g in range(groups)], 0
        )
        out[...] = jnp.dot(block, scaled, preferred_element_type=F32).astype(out.dtype)


def partial_keys(tokens, weight, count):
    rows, width = tokens.shape[0] // count, weight.shape[1]
    return pl.pallas_call(
        partial_kernel,
        out_shape=[like((rows, width))] * count,
        in_specs=[SMEM, VMEM, VMEM],
        out_specs=[VMEM] * count,
        compiler_params=params(16),
        cost_estimate=BRIEF,
    )(lax.axis_index("x").reshape(1), tokens, weight)


def ring_sum_kernel(me_ref, after_ref, *refs):
    parts, outs, token_ref = refs[:-4], refs[-4:-1], refs[-1]
    token_ref[...] = jnp.zeros(token_ref.shape, F32)
    count = len(outs)
    rows = outs[0].shape[0]
    for shift, out in enumerate(outs):
        at = pl.ds(pl.multiple_of(lax.rem(me_ref[0] + shift, count) * rows, rows), rows)
        total = parts[0][at, :].astype(F32)
        for part in parts[1:]:
            total = total + part[at, :].astype(F32)
        out[...] = total.astype(out.dtype)


def ring_sum(parts, token):
    rows, width = parts[0].shape
    return pl.pallas_call(
        ring_sum_kernel,
        out_shape=[like((rows // 3, width), F32)] + [like((rows // 3, width))] * 2 + [TOKEN],
        in_specs=[SMEM, ANY] + [VMEM] * len(parts),
        out_specs=[VMEM] * 4,
        compiler_params=params(8),
        cost_estimate=BRIEF,
    )(lax.axis_index("zl").reshape(1), token, *parts)


def pair_kernel(me_ref, grad_ref, got_ref, after_ref, o_ref):
    me = me_ref[0]
    rows = o_ref.shape[0]
    mine = grad_ref[pl.ds(pl.multiple_of(me * rows, rows), rows), :].astype(F32)
    o_ref[...] = (mine + got_ref[1 - me].astype(F32)).astype(o_ref.dtype)


def pair_sum(grad, token):
    rows, width = grad.shape[0] // 2, grad.shape[1]
    core = lax.axis_index("c")
    got = lax.all_gather(lax.dynamic_slice_in_dim(grad, (1 - core) * rows, rows, 0), "c", axis=0)
    return pl.pallas_call(
        pair_kernel,
        out_shape=like((rows, width)),
        in_specs=[SMEM, VMEM, VMEM, ANY],
        out_specs=VMEM,
        compiler_params=params(8),
        cost_estimate=BRIEF,
    )(core.reshape(1), grad, got, token)


def last_sum_kernel(a_ref, b_ref, c_ref, after_ref, o_ref):
    o_ref[...] = (a_ref[...] + b_ref[...].astype(F32) + c_ref[...].astype(F32)).astype(o_ref.dtype)


def last_sum(a, b, c, token):
    return pl.pallas_call(
        last_sum_kernel,
        out_shape=like(a.shape),
        in_specs=[VMEM] * 3 + [ANY],
        out_specs=VMEM,
        compiler_params=params(4),
        cost_estimate=BRIEF,
    )(a, b, c, token)


def send(x, axis, shift):
    count = lax.axis_size(axis)
    return lax.ppermute(x, axis, [(i, (i + shift) % count) for i in range(count)])


def back_kernel(after_ref, piece_ref, weight_ref, o_ref, token_ref, scaled_ref):
    @pl.when(pl.program_id(0) == 0)
    def _():
        scaled_ref[...] = (weight_ref[...] * FACTOR).astype(BF16)
        token_ref[...] = jnp.zeros(token_ref.shape, F32)

    o_ref[...] = lax.dot_general(
        piece_ref[...], scaled_ref[...], (((1,), (1,)), ((), ())), preferred_element_type=F32
    ).astype(o_ref.dtype)


def token_gradient(piece, weight, token):
    rows, width = piece.shape
    feats = weight.shape[0]
    tile = 512
    return pl.pallas_call(
        back_kernel,
        out_shape=[like((rows, feats)), TOKEN],
        grid=(rows // tile,),
        in_specs=[
            ANY,
            pl.BlockSpec((tile, width), lambda i: (i, 0)),
            pl.BlockSpec((feats, width), lambda i: (0, 0)),
        ],
        out_specs=[pl.BlockSpec((tile, feats), lambda i: (i, 0)), pl.BlockSpec((8, 128), lambda i: (0, 0))],
        scratch_shapes=[pltpu.VMEM((feats, width), BF16)],
        compiler_params=params(16),
        cost_estimate=BRIEF,
    )(token, piece, weight)


def local(tokens, key_grad, weight, moment, second):
    rows, width, feats = tokens.shape[0], key_grad.shape[1], tokens.shape[1]
    size = lax.axis_size
    piece = swap_parts(copies_of(key_grad, size("zl") * size("x")), BLK).reshape(rows, width)

    grad = lax.dot_general(tokens, piece, (((0,), (0,)), ((), ())), preferred_element_type=F32) * FACTOR
    grad = grad.astype(BF16)
    own, *out = partial_keys(tokens, weight, size("x"))
    got = [send(x, "x", 1 + i) for i, x in enumerate(out)]
    pair = pair_sum(grad, got[0])
    shares = swap_parts(pair.reshape(size("y"), -1, width), "y")
    shares, first = sum_copies(shares, size("zh"))
    back, after_back = token_gradient(piece, weight, first)
    mine, *out, after_keys = ring_sum([own] + got, first)
    got = [send(x, "zl", 1 + i) for i, x in enumerate(out)]
    shares, _ = sum_copies(swap_parts(shares, "zh"), size("y"), after_back, after_keys)
    half = swap_parts(shares, "y").reshape(pair.shape)
    weight_grad = lax.all_gather(half, "c", axis=0, tiled=True).astype(F32)

    keys = last_sum(mine, *got, half)
    weight_new, moment_new, second_new = optimize(weight, moment, second, weight_grad)
    return (keys, back, weight_grad, weight_new, moment_new, second_new)


def solution(mesh):
    fine = Mesh(mesh.devices.reshape(8, 4, 2, 3, 4), AXES)
    in_specs = (P(DP, BLK), P(DP + BLK, None), P(BLK, None), P(BLK, None), P(BLK, None))
    out_specs = (P(DP + BLK, None), P(DP, BLK), P(BLK, None), P(BLK, None), P(BLK, None), P(BLK, None))
    return jax.shard_map(local, mesh=fine, in_specs=in_specs, out_specs=out_specs, check_vma=False)
```

```python
import jax
import jax.numpy as jnp
from jax import lax
from jax.experimental import pallas as pl
from jax.experimental.pallas import tpu as pltpu
from jax.sharding import Mesh, PartitionSpec as P

D = 6144
STEP = 100
FACTOR = D ** (-0.5)
AXES = ("y", "zh", "c", "zl", "x")
DP = ("y", "zh", "c")
BLK = ("zl", "x")
CROSS = ("x", "zl")
BRIEF = pl.CostEstimate(flops=1, bytes_accessed=1, transcendentals=0)
BF16, F32 = jnp.bfloat16, jnp.float32
VMEM = pl.BlockSpec(memory_space=pltpu.VMEM)
SMEM = pl.BlockSpec(memory_space=pltpu.SMEM)
ANY = pl.BlockSpec(memory_space=pl.ANY)


def optimize(weight, moment, second, weight_grad):
    moment_new = 0.9 * moment + 0.1 * weight_grad
    second_new = 0.999 * second + 0.001 * weight_grad * weight_grad
    first_fix = 1.0 / (1.0 - 0.9**STEP)
    second_fix = 1.0 / (1.0 - 0.999**STEP)
    step_dir = moment_new * first_fix / (jnp.sqrt(second_new * second_fix) + 1e-08)
    weight_new = weight - 0.05 * (step_dir + 0.1 * weight)
    return (weight_new, moment_new, second_new)


def params(mib):
    return pltpu.CompilerParams(vmem_limit_bytes=mib << 20)


def like(shape, dtype=BF16):
    return jax.ShapeDtypeStruct(shape, dtype)


TOKEN = like((8, 128), F32)


def swap_parts(x, axes):
    return lax.all_to_all(x, axes, 0, 0, tiled=True)


def copies_kernel(x_ref, o_ref):
    for i in range(o_ref.shape[0]):
        o_ref[i] = x_ref[...]


def copies_of(x, count):
    return pl.pallas_call(
        copies_kernel,
        out_shape=like((count,) + x.shape, x.dtype),
        in_specs=[VMEM],
        out_specs=VMEM,
        compiler_params=params(4),
        cost_estimate=BRIEF,
    )(x)


def sum_copies_kernel(x_ref, *refs):
    o_ref, token_ref = refs[-2:]
    total = x_ref[0].astype(F32)
    for i in range(1, x_ref.shape[0]):
        total = total + x_ref[i].astype(F32)
    total = total.astype(o_ref.dtype)
    for i in range(o_ref.shape[0]):
        o_ref[i] = total
    token_ref[...] = jnp.zeros(token_ref.shape, F32)


def sum_copies(x, count, *tokens):
    return pl.pallas_call(
        sum_copies_kernel,
        out_shape=[like((count,) + x.shape[1:]), TOKEN],
        in_specs=[VMEM] + [ANY] * len(tokens),
        out_specs=[VMEM] * 2,
        compiler_params=params(4),
        cost_estimate=BRIEF,
    )(x, *tokens)


def partial_kernel(me_ref, tokens_ref, weight_ref, held_ref, *outs):
    count = len(outs)
    groups = 3
    rows = tokens_ref.shape[0] // (count * groups)
    for x in range(count):
        for g in range(groups):
            to, at = (x * groups + g) * rows, (g * count + x) * rows
            held_ref[to : to + rows, :] = tokens_ref[at : at + rows, :]
    scaled = (weight_ref[...] * FACTOR).astype(BF16)
    for shift, out in enumerate(outs):
        at = lax.rem(me_ref[0] + shift, count)
        block = jnp.concatenate(
            [tokens_ref[pl.ds(pl.multiple_of((g * count + at) * rows, rows), rows), :] for g in range(groups)], 0
        )
        out[...] = jnp.dot(block, scaled, preferred_element_type=F32).astype(out.dtype)


def partial_keys(tokens, weight, count):
    rows, width = tokens.shape[0] // count, weight.shape[1]
    return pl.pallas_call(
        partial_kernel,
        out_shape=[like(tokens.shape)] + [like((rows, width))] * count,
        in_specs=[SMEM, VMEM, VMEM],
        out_specs=[VMEM] * (count + 1),
        compiler_params=params(16),
        cost_estimate=BRIEF,
    )(lax.axis_index("x").reshape(1), tokens, weight)


def ring_sum_kernel(me_ref, after_ref, *refs):
    parts, outs, token_ref = refs[:-4], refs[-4:-1], refs[-1]
    token_ref[...] = jnp.zeros(token_ref.shape, F32)
    count = len(outs)
    rows = outs[0].shape[0]
    for shift, out in enumerate(outs):
        at = pl.ds(pl.multiple_of(lax.rem(me_ref[0] + shift, count) * rows, rows), rows)
        total = parts[0][at, :].astype(F32)
        for part in parts[1:]:
            total = total + part[at, :].astype(F32)
        out[...] = total.astype(out.dtype)


def ring_sum(parts, token):
    rows, width = parts[0].shape
    return pl.pallas_call(
        ring_sum_kernel,
        out_shape=[like((rows // 3, width), F32)] + [like((rows // 3, width))] * 2 + [TOKEN],
        in_specs=[SMEM, ANY] + [VMEM] * len(parts),
        out_specs=[VMEM] * 4,
        compiler_params=params(8),
        cost_estimate=BRIEF,
    )(lax.axis_index("zl").reshape(1), token, *parts)


def pair_kernel(me_ref, grad_ref, got_ref, after_ref, o_ref):
    me = me_ref[0]
    rows = o_ref.shape[0]
    mine = grad_ref[pl.ds(pl.multiple_of(me * rows, rows), rows), :].astype(F32)
    o_ref[...] = (mine + got_ref[1 - me].astype(F32)).astype(o_ref.dtype)


def pair_sum(grad, token):
    rows, width = grad.shape[0] // 2, grad.shape[1]
    core = lax.axis_index("c")
    got = lax.all_gather(lax.dynamic_slice_in_dim(grad, (1 - core) * rows, rows, 0), "c", axis=0)
    return pl.pallas_call(
        pair_kernel,
        out_shape=like((rows, width)),
        in_specs=[SMEM, VMEM, VMEM, ANY],
        out_specs=VMEM,
        compiler_params=params(8),
        cost_estimate=BRIEF,
    )(core.reshape(1), grad, got, token)


def last_sum_kernel(a_ref, b_ref, c_ref, after_ref, o_ref):
    o_ref[...] = (a_ref[...] + b_ref[...].astype(F32) + c_ref[...].astype(F32)).astype(o_ref.dtype)


def last_sum(a, b, c, token):
    return pl.pallas_call(
        last_sum_kernel,
        out_shape=like(a.shape),
        in_specs=[VMEM] * 3 + [ANY],
        out_specs=VMEM,
        compiler_params=params(4),
        cost_estimate=BRIEF,
    )(a, b, c, token)


def send(x, axis, shift):
    count = lax.axis_size(axis)
    return lax.ppermute(x, axis, [(i, (i + shift) % count) for i in range(count)])


def back_kernel(after_ref, piece_ref, weight_ref, o_ref, token_ref, scaled_ref):
    @pl.when(pl.program_id(0) == 0)
    def _():
        scaled_ref[...] = (weight_ref[...] * FACTOR).astype(BF16)
        token_ref[...] = jnp.zeros(token_ref.shape, F32)

    o_ref[...] = lax.dot_general(
        piece_ref[...].reshape(o_ref.shape[0], -1), scaled_ref[...], (((1,), (1,)), ((), ())), preferred_element_type=F32
    ).astype(o_ref.dtype)


def token_gradient(piece, weight, token):
    wide, tall, own, width = piece.shape
    feats = weight.shape[0]
    rows, tile = wide * tall * own, wide * own
    return pl.pallas_call(
        back_kernel,
        out_shape=[like((rows, feats)), TOKEN],
        grid=(rows // tile,),
        in_specs=[
            ANY,
            pl.BlockSpec((wide, 1, own, width), lambda i: (0, i, 0, 0)),
            pl.BlockSpec((feats, width), lambda i: (0, 0)),
        ],
        out_specs=[pl.BlockSpec((tile, feats), lambda i: (i, 0)), pl.BlockSpec((8, 128), lambda i: (0, 0))],
        scratch_shapes=[pltpu.VMEM((feats, width), BF16)],
        compiler_params=params(16),
        cost_estimate=BRIEF,
    )(token, piece, weight)


def local(tokens, key_grad, weight, moment, second):
    rows, width, feats = tokens.shape[0], key_grad.shape[1], tokens.shape[1]
    size = lax.axis_size
    piece = swap_parts(copies_of(key_grad, size("zl") * size("x")), CROSS).reshape(rows, width)

    held, own, *out = partial_keys(tokens, weight, size("x"))
    grad = lax.dot_general(held, piece, (((0,), (0,)), ((), ())), preferred_element_type=F32) * FACTOR
    grad = grad.astype(BF16)
    got = [send(x, "x", 1 + i) for i, x in enumerate(out)]
    pair = pair_sum(grad, got[0])
    shares = swap_parts(pair.reshape(size("y"), -1, width), "y")
    shares, first = sum_copies(shares, size("zh"))
    back, after_back = token_gradient(piece.reshape(size("x"), size("zl"), -1, width), weight, first)
    mine, *out, after_keys = ring_sum([own] + got, first)
    got = [send(x, "zl", 1 + i) for i, x in enumerate(out)]
    shares, _ = sum_copies(swap_parts(shares, "zh"), size("y"), after_back, after_keys)
    half = swap_parts(shares, "y").reshape(pair.shape)
    weight_grad = lax.all_gather(half, "c", axis=0, tiled=True).astype(F32)

    keys = last_sum(mine, *got, half)
    weight_new, moment_new, second_new = optimize(weight, moment, second, weight_grad)
    return (keys, back, weight_grad, weight_new, moment_new, second_new)


def solution(mesh):
    fine = Mesh(mesh.devices.reshape(8, 4, 2, 3, 4), AXES)
    in_specs = (P(DP, BLK), P(DP + BLK, None), P(BLK, None), P(BLK, None), P(BLK, None))
    out_specs = (P(DP + BLK, None), P(DP, BLK), P(BLK, None), P(BLK, None), P(BLK, None), P(BLK, None))
    return jax.shard_map(local, mesh=fine, in_specs=in_specs, out_specs=out_specs, check_vma=False)
```
